128 devices in a mesh: row: 8 (over x, core), col: 16 (over z, y).
Axes of the slice: x: 4, y: 4, z: 4, core: 2. Of those that a mesh axis runs over, the one named last changes fastest.
Arguments:
- tiles: bfloat16 [128, 64, 128, 128], P(('row', 'col')), may hold values from -6 to 6
- tile_mu: int32 [128], P(('row', 'col')), may hold values from 0 to 1
- tile_nu: int32 [128], P(('row', 'col')), may hold values from 0 to 7, as said below
- orbitals: bfloat16 [8192, 4096], P('row', 'col'), may hold values from -0.0625 to 0.0625
- metric_inverse: float32 [2, 64, 64], replicated, may hold values from -1 to 2, as said below
Outputs:
- fitted: bfloat16 [2, 64, 128, 4096], P(None, None, 'row', 'col')
- exchange: float32 [2, 128, 128], P(None, 'row')
The draws below stay inside these ranges and needn't reach their ends.
Inputs may be any that keep to these rules, and one draw needn't show every extreme that they name: Within one grid row no two blocks have both the same tile_mu and the same tile_nu. `metric_inverse`: symmetric in its last two dimensions.
All inputs are finite; a program needn't handle non-finite values.
Results may differ from the reference program's by a relative error of at most 0.02.
Values may be sent and summed in bfloat16 or wider, within the bound.
No kernel may reach another device: no remote copies, remote signals or barrier semaphores. Data moves between devices by JAX's collectives and lax.ppermute only.
A program may use at most 192 MiB of HBM per device.

```python
import math
import jax
import jax.numpy as jnp
from jax import lax

FN = 128
AUX = 64
MB = 2
NB_ROW = 8
TILES = 128
OCCW = 4096
NB = 64
N_ROW = 8


def pair_slots(key):
    per_row = TILES // N_ROW
    row_keys = jax.random.split(key, N_ROW)

    def one_row(row_key):
        return jax.random.permutation(row_key, MB * NB_ROW)[:per_row]
    return jax.vmap(one_row)(row_keys).reshape(-1).astype(jnp.int32)


def draw_tile_mu(key, part):
    slots = pair_slots(key)
    return (slots // NB_ROW).astype(jnp.int32)


def draw_tile_nu(key, part):
    slots = pair_slots(key)
    return (slots % NB_ROW).astype(jnp.int32)


def draw_metric_inverse(key, part):
    key = jax.random.fold_in(key, 5)
    noise_key, diag_key = jax.random.split(key, 2)
    noise = jax.random.normal(noise_key, (MB, AUX, AUX), jnp.float32) * (0.6 / math.sqrt(AUX))
    paired = (noise + jnp.swapaxes(noise, 1, 2)) * 0.7071
    diagonal = jax.random.uniform(diag_key, (MB, AUX), jnp.float32, 0.5, 2.0)
    identity = jnp.eye(AUX, dtype=jnp.float32)
    return paired * (1.0 - identity) + identity * diagonal[:, :, None]


def levels(key, shape, cuts, smallest, top_value):
    level = 1.0
    for axis_at, blocks in cuts:
        heights = jax.random.uniform(jax.random.fold_in(jax.random.fold_in(key, 6), axis_at), (blocks,), jnp.float32, smallest / len(cuts), top_value / len(cuts))
        level = level * jnp.repeat(jnp.exp(heights), shape[axis_at] // blocks).reshape((-1,) + (1,) * (len(shape) - 1 - axis_at))
    return level


def gaussian(own_key, dims, deviation, limit, shards=(), kind=jnp.bfloat16):
    values = deviation * jax.random.normal(own_key, dims, jnp.float32)
    if shards:
        values = values * levels(own_key, dims, shards, -0.22, 0.18)
    return jnp.clip(values, -limit, limit).astype(kind)


def setup_inputs(seed: int = 0) -> dict:
    seeds = jax.random.split(jax.random.key(seed), 6)
    tiles = gaussian(seeds[0], (TILES, AUX, FN, FN), 1.0, 6.0, ((0, 128),))
    tile_mu = draw_tile_mu(jax.random.fold_in(seeds[5], 71), 0)
    tile_nu = draw_tile_nu(jax.random.fold_in(seeds[5], 71), 0)
    orbitals = gaussian(seeds[3], (NB * FN, OCCW), (FN * TILES // MB) ** -0.5, 0.0625, ((0, 8), (1, 16)))
    metric_inverse = draw_metric_inverse(jax.random.fold_in(seeds[5], 71), 0)
    return dict(tiles=tiles, tile_mu=tile_mu, tile_nu=tile_nu, orbitals=orbitals, metric_inverse=metric_inverse)


def reference(tiles, tile_mu, tile_nu, orbitals, metric_inverse):
    per_row = TILES // N_ROW
    row_tiles = tiles.reshape(N_ROW, per_row, AUX, FN, FN)
    row_mu = tile_mu.reshape(N_ROW, per_row)
    row_nu = tile_nu.reshape(N_ROW, per_row)
    row_blocks = orbitals.reshape(N_ROW, NB_ROW, FN, OCCW)

    def row_partial(total, row):
        tile_set, mu_set, nu_set, block_set = row

        def add_tile(acc, item):
            tile, mu_index, nu_index = item
            block = lax.dynamic_index_in_dim(block_set, nu_index.astype(jnp.int32), 0, keepdims=False)
            product = jnp.dot(tile.reshape(AUX * FN, FN), block, preferred_element_type=jnp.float32)
            product = lax.optimization_barrier(product.astype(jnp.bfloat16)).reshape(AUX, FN, OCCW)
            current = lax.dynamic_index_in_dim(acc, mu_index.astype(jnp.int32), 0, keepdims=False)
            updated = current + product.astype(jnp.float32)
            return lax.dynamic_update_index_in_dim(acc, updated, mu_index.astype(jnp.int32), 0), None

        start = jnp.zeros((MB, AUX, FN, OCCW), jnp.float32)
        partial_value, _ = lax.scan(add_tile, start, (tile_set, mu_set, nu_set))
        rounded = lax.optimization_barrier(partial_value.astype(jnp.bfloat16))
        return total + rounded.astype(jnp.float32), None

    total, _ = lax.scan(row_partial, jnp.zeros((MB, AUX, FN, OCCW), jnp.float32),
                        (row_tiles, row_mu, row_nu, row_blocks))
    coeffs = total.astype(jnp.bfloat16)
    fitted = jnp.einsum("mqp,mpxi->mqxi", metric_inverse, coeffs.astype(jnp.float32),
                        precision=lax.Precision.HIGHEST).astype(jnp.bfloat16)
    exchange = jnp.einsum("mqxi,mqyi->mxy", fitted.astype(jnp.float32), coeffs.astype(jnp.float32)) / (AUX * OCCW)
    return fitted, exchange
```

```python
import functools

import jax
import jax.numpy as jnp
from jax import lax
from jax.experimental import pallas as pl
from jax.experimental.pallas import tpu as pltpu
from jax.sharding import PartitionSpec as P

F32 = jnp.float32
BF16 = jnp.bfloat16

CHUNKS = (4, 4, 4, 4)

VMEM = pl.BlockSpec(memory_space=pltpu.VMEM)
SMEM = pl.BlockSpec(memory_space=pltpu.SMEM)


def shift_x(value, step):
    return lax.ppermute(value, "row", [(2 * x + k, 2 * ((x + step) % 4) + k) for x in range(4) for k in range(2)])


def swap_core(value):
    return lax.ppermute(value, "row", [(r, r ^ 1) for r in range(8)])


def shift_y(value, step):
    return lax.ppermute(value, "col", [(4 * z + y, 4 * z + (y + step) % 4) for z in range(4) for y in range(4)])


def shift_z(value, step):
    return lax.ppermute(value, "col", [(4 * z + y, 4 * ((z + step) % 4) + y) for z in range(4) for y in range(4)])


def call(body, out_shape, in_specs, name, scratch=(), flops=0, nbytes=0, limit=48):
    return pl.pallas_call(
        body,
        out_shape=out_shape,
        in_specs=in_specs,
        out_specs=jax.tree.map(lambda _: VMEM, out_shape),
        scratch_shapes=list(scratch),
        name=name,
        compiler_params=pltpu.CompilerParams(vmem_limit_bytes=limit * 1024 * 1024),
        cost_estimate=pl.CostEstimate(flops=flops, bytes_accessed=nbytes, transcendentals=0),
    )


def relayout_body(parts, y_ref, x_ref, *refs):
    outs, wide = refs[:-1], refs[-1]
    wide[...] = x_ref[...].reshape(wide.shape).astype(F32)
    for (offset, count), out in zip(parts, outs):
        for k in range(2):
            for x in range(4):
                for uu in range(count):
                    u = 16 * (2 * x + k) + offset + uu
                    row = (k * 4 + x) * count + uu
                    out[0, row] = wide[pl.ds(u, 16, stride=128), :].astype(BF16)


def relayout(tile, y, parts):
    def block(step, y_ref):
        return ((step + y_ref[0]) % 4, 0, 0)

    return pl.pallas_call(
        functools.partial(relayout_body, parts),
        grid_spec=pltpu.PrefetchScalarGridSpec(
            num_scalar_prefetch=1,
            grid=(4,),
            in_specs=[pl.BlockSpec((16, 128, 128), block)],
            out_specs=[
                pl.BlockSpec((1, 8 * count, 16, 128), lambda step, y_ref: (step, 0, 0, 0)) for _, count in parts
            ],
            scratch_shapes=[pltpu.VMEM((2048, 128), F32)],
        ),
        out_shape=[jax.ShapeDtypeStruct((4, 8 * count, 16, 128), BF16) for _, count in parts],
        name="relayout",
        compiler_params=pltpu.CompilerParams(vmem_limit_bytes=32 * 1024 * 1024),
        cost_estimate=pl.CostEstimate(flops=0, bytes_accessed=4 << 20, transcendentals=0),
    )(y, tile)


def product_body(count, code_ref, xk_ref, t0, t1, t2, t3, t4, o0, o1, o2, o3, own, peer, rows):
    rp = 16 * count
    x, k = xk_ref[0], xk_ref[1]
    tiles = [(t, i) for t in (t0, t1, t2, t3, t4) for i in range(t.shape[0])]
    for index, (ref, i) in enumerate(tiles):
        code = code_ref[index]
        m = code // 8
        lane = pl.multiple_of((code % 8) * 128, 128)
        for h in range(2):
            for e in range(4):
                source = pl.multiple_of((((k + h) % 2) * 4 + (x + e) % 4) * rp, rp)
                place = (h * 4 + e) * rp
                rows[m, place:place + rp, pl.ds(lane, 128)] = ref[i, pl.ds(source, rp), :]
    for h, out in ((1, peer), (0, own)):
        for d, orb in enumerate((o0, o1, o2, o3)):
            for m in range(2):
                acc = jnp.dot(rows[m, h * 4 * rp:(h + 1) * 4 * rp, :], orb[...], preferred_element_type=F32)
                for e in range(4):
                    out[e, d, m] = acc[e * rp:(e + 1) * rp].astype(BF16)


def product(count, code, xk, tiles, orbs):
    rp = 16 * count
    shape = jax.ShapeDtypeStruct((4, 4, 2, rp, 256), BF16)
    return call(
        functools.partial(product_body, count),
        [shape, shape],
        [SMEM, SMEM] + [VMEM] * 9,
        "product",
        scratch=[pltpu.VMEM((2, 8 * rp, 1024), BF16)],
        flops=2 * 2 * 8 * rp * 1024 * 1024,
        nbytes=6 << 20,
    )(code, xk, *tiles, *orbs)


def pair_body(a, b, *outs):
    for e, out in enumerate(outs):
        out[...] = (a[e + 1].astype(F32) + b[e + 1].astype(F32)).astype(BF16)


def total_body(a, b, j1, j2, j3, *outs):
    for d, out in enumerate(outs):
        value = a[0, d].astype(F32) + b[0, d].astype(F32)
        value = value + j1[d].astype(F32) + j2[d].astype(F32) + j3[d].astype(F32)
        out[...] = value.astype(BF16)


def fit_body(count, xky_ref, c0, c1, c2, c3, metric, fitted, s0, s1, s2, s3, coef, fit):
    x, k, y = xky_ref[0], xky_ref[1], xky_ref[2]
    for d, ref in enumerate((c0, c1, c2, c3)):
        row = pl.multiple_of(((y + d) % 4) * 16, 16)
        for m in range(2):
            for uu in range(count):
                coef[m, pl.ds(row, 16), uu * 256:(uu + 1) * 256] = ref[m, uu * 16:(uu + 1) * 16, :]
    for m in range(2):
        high = metric[m].astype(BF16)
        low = (metric[m] - high.astype(F32)).astype(BF16)
        both = jnp.concatenate([high, low], axis=1)
        value = coef[m]
        fit[m] = jnp.dot(both, jnp.concatenate([value, value], axis=0), preferred_element_type=F32).astype(BF16)
    fitted[...] = fit[...]
    for e, out in enumerate((s0, s1, s2, s3)):
        for h in range(2):
            r = 2 * ((x + e) % 4) + (k + h) % 2
            q = pl.multiple_of((r % 4) * 16, 16)
            out[h, 0] = fit[r // 4, pl.ds(q, 16), :]
            out[h, 1] = coef[r // 4, pl.ds(q, 16), :]


def fit_part(count, xky, pieces, metric):
    lanes = 256 * count
    shape = jax.ShapeDtypeStruct((2, 64, lanes), BF16)
    send = jax.ShapeDtypeStruct((2, 2, 16, lanes), BF16)
    return call(
        functools.partial(fit_body, count),
        [shape, send, send, send, send],
        [SMEM] + [VMEM] * 5,
        "fit",
        scratch=[pltpu.VMEM((2, 64, lanes), BF16), pltpu.VMEM((2, 64, lanes), BF16)],
        flops=2 * 2 * 64 * 128 * lanes,
        nbytes=1 << 20,
    )(xky, *pieces, metric)


def assemble_body(parts, *refs):
    out = refs[-1]
    for (offset, count), ref in zip(parts, refs[:-1]):
        for uu in range(count):
            for m in range(2):
                out[m, :, offset + uu, :] = ref[m, :, uu * 256:(uu + 1) * 256]


def exchange_body(parts, xk_ref, *refs):
    out, *wides = refs[-5:]
    x, k = xk_ref[0], xk_ref[1]
    refs = refs[:-5]
    for part, (offset, count) in enumerate(parts):
        near = refs[5 * part:5 * part + 4]
        far = refs[5 * part + 4]
        for e in range(4):
            for h in range(2):
                r = 2 * ((x - e + 4) % 4) + (k + h) % 2
                for uu in range(count):
                    row = pl.multiple_of((16 * r + offset + uu) * 16, 16)
                    for index, wide in enumerate(wides):
                        which, lane = index // 2, uu * 256 + index % 2 * 128
                        lanes = slice(lane, lane + 128)
                        value = near[e][0, which, :, lanes] if h == 0 else far[e, which, :, lanes]
                        wide[pl.ds(row, 16), :] = value.astype(F32)
    acc = jnp.zeros((128, 128), F32)
    for q in range(16):
        halves = [wide[pl.ds(q, 128, stride=16), :].astype(BF16) for wide in wides]
        a = jnp.concatenate(halves[:2], axis=1)
        b = jnp.concatenate(halves[2:], axis=1)
        acc = acc + lax.dot_general(a, b, (((1,), (1,)), ((), ())), preferred_element_type=F32)
    out[...] = acc


def on_device(tiles, tile_mu, tile_nu, orbitals, metric_inverse):
    row = lax.axis_index("row").astype(jnp.int32)
    col = lax.axis_index("col").astype(jnp.int32)
    x, k, y = row // 2, row % 2, col % 4
    xk = jnp.stack([x, k])
    xky = jnp.stack([x, k, y])
    offsets = [sum(CHUNKS[:i]) for i in range(len(CHUNKS))]
    parts = list(zip(offsets, CHUNKS))

    with jax.named_scope("tile_slots"):
        code = tile_mu * 8 + tile_nu
        near = jnp.concatenate([code] + [shift_y(code, d) for d in (1, 2, 3)])
        codes = jnp.concatenate([near, shift_z(near, 1), shift_z(near, 3), shift_z(near, 2)])

    with jax.named_scope("tile_relayout"):
        first = relayout(tiles[0], y.reshape(1), parts[:1])
        rest = relayout(tiles[0], y.reshape(1), parts[1:])
        laid = list(first) + list(rest)

    with jax.named_scope("orbital_gather"):
        orbs = [orbitals] + [shift_y(orbitals, d) for d in (1, 2, 3)]

    fitted_parts, pieces = [], []
    for (offset, count), own in zip(parts, laid):
        rows = 8 * count * 16
        with jax.named_scope("tiles_over_y"):
            shard = jnp.stack([own[0]] + [shift_y(own[d], d) for d in (1, 2, 3)]).reshape(4, rows, 128)
        with jax.named_scope("tiles_over_z"):
            below = shift_z(shard, 1)
            above = shift_z(shard, 3)
            far_low = shift_z(below[:2], 1)
            far_high = shift_z(above[2:], 3)
        with jax.named_scope("products"):
            mine, others = product(count, codes, xk, (shard, below, above, far_low, far_high), orbs)
        with jax.named_scope("sum_cores"):
            twin = swap_core(others)
            shape = jax.ShapeDtypeStruct(mine.shape[1:], BF16)
            sends = call(pair_body, [shape] * 3, [VMEM] * 2, "pair", nbytes=3 << 20)(mine, twin)
        with jax.named_scope("sum_x"):
            got = [shift_x(send, e + 1) for e, send in enumerate(sends)]
            shape = jax.ShapeDtypeStruct(mine.shape[2:], BF16)
            blocks = call(total_body, [shape] * 4, [VMEM] * 5, "total", nbytes=2 << 20)(mine, twin, *got)
        with jax.named_scope("coeffs_over_y"):
            blocks = [blocks[0]] + [shift_y(blocks[d], -d) for d in (1, 2, 3)]
        with jax.named_scope("fit"):
            fit, *sends = fit_part(count, xky, blocks, metric_inverse)
            fitted_parts.append(fit)
        with jax.named_scope("exchange_over_row"):
            arrived = [sends[0]] + [shift_x(sends[e], e) for e in (1, 2, 3)]
            pieces += arrived + [swap_core(jnp.stack([part[1] for part in arrived]))]

    with jax.named_scope("fitted_out"):
        fitted = call(
            functools.partial(assemble_body, parts),
            jax.ShapeDtypeStruct((2, 64, 16, 256), BF16),
            [VMEM] * len(parts),
            "assemble",
            nbytes=2 << 20,
        )(*fitted_parts)

    with jax.named_scope("exchange"):
        block = call(
            functools.partial(exchange_body, parts),
            jax.ShapeDtypeStruct((128, 128), F32),
            [SMEM] + [VMEM] * len(pieces),
            "exchange",
            scratch=[pltpu.VMEM((2048, 128), F32)] * 4,
            flops=2 * 128 * 128 * 4096,
            nbytes=2 << 20,
        )(xk, *pieces)
        block = block.reshape(4, 32, 128)
        total = jnp.zeros((2, 32, 128), F32)
        for e in range(4):
            value = lax.dynamic_index_in_dim(block, (x + e) % 4, 0, keepdims=False)
            value = value if e == 0 else shift_x(value, e)
            source = (x - e) % 4
            total = total + jnp.where((source // 2 == jnp.arange(2))[:, None, None], value[None], 0.0)
        total = total.reshape(2, 2, 16, 128)
        keep = lax.dynamic_index_in_dim(total, k, 1, keepdims=False)
        give = lax.dynamic_index_in_dim(total, 1 - k, 1, keepdims=False)
        total = keep + swap_core(give)
        for shift in (shift_y, shift_z):
            total = total + (shift(total, 1) + shift(total, 2) + shift(total, 3))
        exchange = total / 262144.0
    return fitted, exchange


def solution(mesh):
    return jax.shard_map(
        on_device,
        mesh=mesh,
        in_specs=(
            P(("row", "col"), None, None, None),
            P(("row", "col")),
            P(("row", "col")),
            P("row", "col"),
            P(),
        ),
        out_specs=(P(None, None, "row", "col"), P(None, "row", None)),
        check_vma=False,
    )
```

```python
import functools

import jax
import jax.numpy as jnp
from jax import lax
from jax.experimental import pallas as pl
from jax.experimental.pallas import tpu as pltpu
from jax.sharding import PartitionSpec as P

F32 = jnp.float32
BF16 = jnp.bfloat16

CHUNKS = (8, 8)

VMEM = pl.BlockSpec(memory_space=pltpu.VMEM)
SMEM = pl.BlockSpec(memory_space=pltpu.SMEM)
ANY = pl.BlockSpec(memory_space=pl.ANY)


def index(x, k, z, y):
    return ((x * 2 + k) * 4 + z) * 4 + y


def move(value, axis, step):
    pairs = []
    for x in range(4):
        for k in range(2):
            for z in range(4):
                for y in range(4):
                    to = dict(x=x, z=z, y=y)
                    to[axis] = (to[axis] + step * (1 - 2 * k)) % 4
                    pairs.append((index(x, k, z, y), index(to["x"], k, to["z"], to["y"])))
    return lax.ppermute(value, ("row", "col"), pairs)


def swap_core(value):
    return lax.ppermute(value, "row", [(r, r ^ 1) for r in range(8)])


def call(body, out_shape, in_specs, name, args, after=(), scratch=(), flops=0, nbytes=0, limit=8):
    given, marks = len(args), [mark(item) for item in after]

    def kernel(*refs):
        body(*refs[:given], *refs[given + len(marks):])

    return pl.pallas_call(
        kernel,
        out_shape=out_shape,
        in_specs=list(in_specs) + [VMEM] * len(marks),
        out_specs=jax.tree.map(lambda _: VMEM, out_shape),
        scratch_shapes=list(scratch),
        name=name,
        compiler_params=pltpu.CompilerParams(vmem_limit_bytes=limit * 1024 * 1024),
        cost_estimate=pl.CostEstimate(flops=flops, bytes_accessed=nbytes, transcendentals=0),
    )(*args, *marks)


def mark(item):
    item = item[(0,) * (item.ndim - 2)]
    return item[:16, :128]


def copy_body(source, out):
    out[...] = source[...]


def gate(value, after):
    shape = jax.ShapeDtypeStruct(value.shape, value.dtype)
    return call(copy_body, shape, [VMEM], "gate", (value,), after, nbytes=2 * value.size * 2)


def relayout_body(parts, yc_ref, x_ref, *refs):
    *orbitals, out, wide = refs
    wide[...] = x_ref[...].reshape(wide.shape).astype(F32)
    row = 0
    for offset, count in parts:
        for r in [2 * x + k for k in range(2) for x in range(4)]:
            for u in range(16 * r + offset, 16 * r + offset + count):
                out[0, row] = wide[pl.ds(u, 16, stride=128), :].astype(BF16)
                row += 1
        out[0, row] = jnp.full((16, 128), yc_ref[2].astype(F32), F32).astype(BF16)
        row += 1
    for ref in orbitals:
        for half in range(2):
            out[0, row:row + 64] = ref[:, half * 128:(half + 1) * 128].reshape(64, 16, 128)
            row += 64


def relayout(tile, yc, parts, orbitals):
    def block(step, yc_ref):
        return ((yc_ref[0] + step * yc_ref[1] + 4) % 4, 0, 0)

    blocks = sum(8 * count + 1 for _, count in parts) + 128 * len(orbitals)
    return pl.pallas_call(
        functools.partial(relayout_body, parts),
        grid_spec=pltpu.PrefetchScalarGridSpec(
            num_scalar_prefetch=1,
            grid=(4,),
            in_specs=[pl.BlockSpec((16, 128, 128), block)] + [VMEM] * len(orbitals),
            out_specs=pl.BlockSpec((1, blocks, 16, 128), lambda step, yc_ref: (step, 0, 0, 0)),
            scratch_shapes=[pltpu.VMEM((2048, 128), F32)],
        ),
        out_shape=jax.ShapeDtypeStruct((4, blocks, 16, 128), BF16),
        name="relayout",
        compiler_params=pltpu.CompilerParams(vmem_limit_bytes=8 * 1024 * 1024),
        cost_estimate=pl.CostEstimate(flops=0, bytes_accessed=4 << 20, transcendentals=0),
    )(yc, tile, *orbitals)


def stack_body(start, first, a, b, c, out):
    blocks = out.shape[1] // 16
    out[0] = first[0, start:start + blocks].reshape(out.shape[1:])
    for i, ref in enumerate((a, b, c)):
        out[i + 1] = ref[start:start + blocks].reshape(out.shape[1:])


def product_body(count, xky_ref, t0, t1, t2, t3, orb, o1, o2, o3, own, peer, rows, orbs):
    rp = 16 * count
    x, k, sign = xky_ref[0], xky_ref[1], xky_ref[2]
    for ref in (t0, t1, t2, t3):
        for i in range(4):
            code = jnp.max(ref[i, 8 * rp:8 * rp + 16, :].astype(F32)).astype(jnp.int32)
            m = code >> 3
            lane = pl.multiple_of((code & 7) * 128, 128)
            for h in range(2):
                for e in range(4):
                    towards = (x + sign * e + 4) % 4 if h == 0 else (x - sign * e + 4) % 4
                    source = pl.multiple_of((((k + h) % 2) * 4 + towards) * rp, rp)
                    place = (h * 4 + e) * rp
                    rows[m, place:place + rp, pl.ds(lane, 128)] = ref[i, pl.ds(source, rp), :]
    orbs[0] = orb[...]
    for d, ref in enumerate((o1, o2, o3)):
        for half in range(2):
            start = ref.shape[0] - 128 + 64 * half
            orbs[d + 1, :, half * 128:(half + 1) * 128] = ref[start:start + 64].reshape(1024, 128)
    for h, out in ((1, peer), (0, own)):
        for d in range(4):
            orb = orbs[d]
            place = d if h == 0 else (4 - d) % 4
            for m in range(2):
                acc = jnp.dot(rows[m, h * 4 * rp:(h + 1) * 4 * rp, :], orb, preferred_element_type=F32)
                for e in range(4):
                    out[e, place, m] = acc[e * rp:(e + 1) * rp].astype(BF16)


def product(count, xky, tiles, orbs, after):
    rp = 16 * count
    shape = jax.ShapeDtypeStruct((4, 4, 2, rp, 256), BF16)
    return call(
        functools.partial(product_body, count),
        [shape, shape],
        [SMEM] + [VMEM] * 8,
        "product",
        (xky, *tiles, *orbs),
        after,
        scratch=[pltpu.VMEM((2, 8 * rp, 1024), BF16), pltpu.VMEM((4, 1024, 256), BF16)],
        flops=2 * 2 * 8 * rp * 1024 * 1024,
        nbytes=6 << 20,
        limit=14,
    )


def pair_body(a, b, *outs):
    for e, out in enumerate(outs):
        out[...] = (a[e + 1].astype(F32) + b[e + 1].astype(F32)).astype(BF16)


def total_body(a, b, j1, j2, j3, *outs):
    for d, out in enumerate(outs):
        value = a[0, d].astype(F32) + b[0, d].astype(F32)
        value = value + j1[d].astype(F32) + j2[d].astype(F32) + j3[d].astype(F32)
        out[...] = value.astype(BF16)


def fit_body(count, xky_ref, c0, c1, c2, c3, metric, fitted, s0, s1, s2, s3, coef, fit):
    x, k, sign, y = xky_ref[0], xky_ref[1], xky_ref[2], xky_ref[3]
    for d, ref in enumerate((c0, c1, c2, c3)):
        row = pl.multiple_of(((y + sign * d + 4) % 4) * 16, 16)
        for m in range(2):
            for uu in range(count):
                coef[m, pl.ds(row, 16), uu * 256:(uu + 1) * 256] = ref[m, uu * 16:(uu + 1) * 16, :]
    for m in range(2):
        high = metric[m].astype(BF16)
        low = (metric[m] - high.astype(F32)).astype(BF16)
        both = jnp.concatenate([high, low], axis=1)
        value = coef[m]
        fit[m] = jnp.dot(both, jnp.concatenate([value, value], axis=0), preferred_element_type=F32).astype(BF16)
    fitted[...] = fit[...]
    for e, out in enumerate((s0, s1, s2, s3)):
        for h in range(2):
            m = (k + h) % 2
            q = pl.multiple_of(((x + sign * e + 4) % 4) * 16, 16)
            out[h, 0] = fit[m, pl.ds(q, 16), :]
            out[h, 1] = coef[m, pl.ds(q, 16), :]


def fit_part(count, xky, pieces, metric, after):
    lanes = 256 * count
    shape = jax.ShapeDtypeStruct((2, 64, lanes), BF16)
    send = jax.ShapeDtypeStruct((2, 2, 16, lanes), BF16)
    return call(
        functools.partial(fit_body, count),
        [shape, send, send, send, send],
        [SMEM] + [VMEM] * 5,
        "fit",
        (xky, *pieces, metric),
        after,
        scratch=[pltpu.VMEM((2, 64, lanes), BF16), pltpu.VMEM((2, 64, lanes), BF16)],
        flops=2 * 2 * 64 * 128 * lanes,
        nbytes=1 << 20,
    )


def assemble_body(parts, *refs):
    out = refs[-1]
    for (offset, count), ref in zip(parts, refs[:-1]):
        for uu in range(count):
            for m in range(2):
                out[m, :, offset + uu, :] = ref[m, :, uu * 256:(uu + 1) * 256]


def exchange_body(parts, xk_ref, *refs):
    *outs, total = refs[-9:-4]
    wides = refs[-4:]
    x, k, sign = xk_ref[0], xk_ref[1], xk_ref[2]
    refs = refs[:-9]
    for part, (offset, count) in enumerate(parts):
        near = refs[5 * part:5 * part + 4]
        far = refs[5 * part + 4]
        for e in range(4):
            for h in range(2):
                source = (x - sign * e + 4) % 4 if h == 0 else (x + sign * e + 4) % 4
                r = 2 * source + (k + h) % 2
                for uu in range(count):
                    row = pl.multiple_of((16 * r + offset + uu) * 16, 16)
                    for index, wide in enumerate(wides):
                        which, lane = index // 2, uu * 256 + index % 2 * 128
                        lanes = slice(lane, lane + 128)
                        value = near[e][0, which, :, lanes] if h == 0 else far[e, which, :, lanes]
                        wide[pl.ds(row, 16), :] = value.astype(F32)
    acc = jnp.zeros((128, 128), F32)
    for q in range(16):
        halves = [wide[pl.ds(q, 128, stride=16), :].astype(BF16) for wide in wides]
        a = jnp.concatenate(halves[:2], axis=1)
        b = jnp.concatenate(halves[2:], axis=1)
        acc = acc + lax.dot_general(a, b, (((1,), (1,)), ((), ())), preferred_element_type=F32)
    total[...] = acc
    for e, out in enumerate(outs):
        out[...] = total[pl.ds(pl.multiple_of(((x + sign * e + 4) % 4) * 32, 32), 32), :]


def on_device(tiles, tile_mu, tile_nu, orbitals, metric_inverse):
    row = lax.axis_index("row").astype(jnp.int32)
    col = lax.axis_index("col").astype(jnp.int32)
    x, k, y = row // 2, row % 2, col % 4
    sign = 1 - 2 * k
    xk = jnp.stack([x, k, sign])
    xky = jnp.stack([x, k, sign, y])
    yc = jnp.stack([y, sign, tile_mu[0] * 8 + tile_nu[0]])
    last = len(CHUNKS) - 1
    offsets = [sum(CHUNKS[:i]) for i in range(len(CHUNKS))]
    parts = list(zip(offsets, CHUNKS))

    shards, gathered, sums, fits = {}, {}, {}, {}
    groups = [parts[:1], parts[1:]]
    spread = []

    def over_y(group, held):
        with jax.named_scope("tiles_over_y"):
            spread.append((held, *[move(held[d], "y", d) for d in (1, 2, 3)]))

    def stack(i, after):
        with jax.named_scope("tiles_over_z"):
            start = 8 * (parts[i][0] - parts[min(i, 1)][0]) + max(i - 1, 0)
            shape = jax.ShapeDtypeStruct((4, (8 * parts[i][1] + 1) * 16, 128), BF16)
            body = functools.partial(stack_body, start)
            shards[i] = call(body, shape, [VMEM] * 4, "stack", spread[min(i, 1)], after, nbytes=1 << 20)

    def gather_z(i, after):
        with jax.named_scope("tiles_over_z"):
            near = gate(move(shards[i], "z", 1), after)
            across = move(gate(shards[i], [near]), "z", 3)
            gathered[i] = (shards[i], near, across, move(near, "z", 1))

    partial, got, blocks, arrived, pieces = {}, {}, {}, {}, {}

    def multiply(i, after):
        with jax.named_scope("products"):
            partial[i] = product(CHUNKS[i], xky, gathered[i], orbs, after)

    def sum_rows(i, after):
        mine, others = partial[i]
        others = gate(others, after) if after else others
        with jax.named_scope("sum_cores"):
            twin = swap_core(others)
            shape = jax.ShapeDtypeStruct(mine.shape[1:], BF16)
            sends = call(pair_body, [shape] * 3, [VMEM] * 2, "pair", (mine, twin), nbytes=3 << 20)
        with jax.named_scope("sum_x"):
            got[i] = (mine, twin, *[move(send, "x", e + 1) for e, send in enumerate(sends)])

    def coeffs(i):
        with jax.named_scope("sum_x"):
            shape = jax.ShapeDtypeStruct(got[i][0].shape[2:], BF16)
            blocks[i] = call(total_body, [shape] * 4, [VMEM] * 5, "total", got[i], nbytes=2 << 20)
        with jax.named_scope("coeffs_over_y"):
            blocks[i] = [blocks[i][0]] + [move(blocks[i][d], "y", -d) for d in (1, 2, 3)]

    def fit(i, after):
        with jax.named_scope("fit"):
            fits[i], *sends = fit_part(CHUNKS[i], xky, blocks[i], metric_inverse, after)
        with jax.named_scope("exchange_over_row"):
            arrived[i] = [sends[0]] + [move(sends[e], "x", e) for e in (1, 2, 3)]
            pieces[i] = arrived[i] + [swap_core(jnp.stack([part[1] for part in arrived[i]]))]

    laid = [relayout(tiles[0], yc, group, held) for group, held in zip(groups, ([], [orbitals]))]
    over_y(groups[0], laid[0])
    stack(0, [laid[1]])
    over_y(groups[1], gate(laid[1], [shards[0]]))
    gather_z(0, [spread[1][3]])
    orbs = [orbitals, *spread[1][1:]]
    for i in range(last + 1):
        if i < last:
            stack(i + 1, gathered[i][2:])
        multiply(i, ([shards[i + 1]] if i < last else []) + (list(got[i - 1][2:4]) if i > 0 else []))
        if i < last:
            gather_z(i + 1, [partial[i][0]])
        sum_rows(i, [gathered[i + 1][1]] if i < last else [])
        if i == 0:
            coeffs(0)
        else:
            coeffs(i)
            fit(i - 1, [blocks[i][0]])
    fit(last, arrived[last - 1][1:3] if last else [])

    with jax.named_scope("fitted_out"):
        fitted = call(
            functools.partial(assemble_body, parts),
            jax.ShapeDtypeStruct((2, 64, 16, 256), BF16),
            [VMEM] * len(parts),
            "assemble",
            [fits[i] for i in range(last + 1)],
            nbytes=2 << 20,
        )

    with jax.named_scope("exchange"):
        pieces = [piece for i in range(last + 1) for piece in pieces[i]]
        blocks = call(
            functools.partial(exchange_body, parts),
            [jax.ShapeDtypeStruct((32, 128), F32)] * 4,
            [SMEM] + [VMEM] * len(pieces),
            "exchange",
            (xk, *pieces),
            scratch=[pltpu.VMEM((128, 128), F32)] + [pltpu.VMEM((2048, 128), F32)] * 4,
            flops=2 * 128 * 128 * 4096,
            nbytes=2 << 20,
        )
        total = blocks[0] + (move(blocks[1], "x", 1) + move(blocks[2], "x", 2) + move(blocks[3], "x", 3))
        keep = jnp.where(k == 0, total[:16], total[16:])
        got = swap_core(jnp.where(k == 0, total[16:], total[:16]))
        total = jnp.stack([jnp.where(k == 0, keep, got), jnp.where(k == 0, got, keep)])
        for axis in ("y", "z"):
            total = total + (move(total, axis, 1) + move(total, axis, 2) + move(total, axis, 3))
        exchange = total / 262144.0
    return fitted, exchange


def solution(mesh):
    return jax.shard_map(
        on_device,
        mesh=mesh,
        in_specs=(
            P(("row", "col"), None, None, None),
            P(("row", "col")),
            P(("row", "col")),
            P("row", "col"),
            P(),
        ),
        out_specs=(P(None, None, "row", "col"), P(None, "row", None)),
        check_vma=False,
    )
```

```python
import functools

import jax
import jax.numpy as jnp
from jax import lax
from jax.experimental import pallas as pl
from jax.experimental.pallas import tpu as pltpu
from jax.sharding import PartitionSpec as P

F32 = jnp.float32
BF16 = jnp.bfloat16

CHUNKS = (8, 8)

VMEM = pl.BlockSpec(memory_space=pltpu.VMEM)
SMEM = pl.BlockSpec(memory_space=pltpu.SMEM)
ANY = pl.BlockSpec(memory_space=pl.ANY)


def index(x, k, z, y):
    return ((x * 2 + k) * 4 + z) * 4 + y


def move(value, axis, step):
    pairs = []
    for x in range(4):
        for k in range(2):
            for z in range(4):
                for y in range(4):
                    to = dict(x=x, z=z, y=y)
                    to[axis] = (to[axis] + step * (1 - 2 * k)) % 4
                    pairs.append((index(x, k, z, y), index(to["x"], k, to["z"], to["y"])))
    return lax.ppermute(value, ("row", "col"), pairs)


def trade(value, axis, mask):
    pairs = [(c, c ^ (mask if axis == "y" else 4 * mask)) for c in range(16)]
    return lax.ppermute(value, "col", pairs)


def swap_core(value):
    return lax.ppermute(value, "row", [(r, r ^ 1) for r in range(8)])


def call(body, out_shape, in_specs, name, args, after=(), scratch=(), flops=0, nbytes=0, limit=8):
    given, marks = len(args), [mark(item) for item in after]

    def kernel(*refs):
        body(*refs[:given], *refs[given + len(marks):])

    return pl.pallas_call(
        kernel,
        out_shape=out_shape,
        in_specs=list(in_specs) + [VMEM] * len(marks),
        out_specs=jax.tree.map(lambda _: VMEM, out_shape),
        scratch_shapes=list(scratch),
        name=name,
        compiler_params=pltpu.CompilerParams(vmem_limit_bytes=limit * 1024 * 1024),
        cost_estimate=pl.CostEstimate(flops=flops, bytes_accessed=nbytes, transcendentals=0),
    )(*args, *marks)


def mark(item):
    item = item[(0,) * (item.ndim - 2)]
    return item[:16, :128]


def copy_body(source, out):
    out[...] = source[...]


def gate(value, after):
    shape = jax.ShapeDtypeStruct(value.shape, value.dtype)
    return call(copy_body, shape, [VMEM], "gate", (value,), after, nbytes=2 * value.size * 2)


def relayout_body(parts, spot_ref, x_ref, *refs):
    *orbitals, out, wide = refs
    wide[...] = x_ref[...].reshape(wide.shape).astype(F32)
    row = 0
    for offset, count in parts:
        for r in [2 * x + k for k in range(2) for x in range(4)]:
            for u in range(16 * r + offset, 16 * r + offset + count):
                out[0, row] = wide[pl.ds(u, 16, stride=128), :].astype(BF16)
                row += 1
        out[0, row] = jnp.full((16, 128), spot_ref[4].astype(F32), F32).astype(BF16)
        row += 1
    for ref in orbitals:
        for half in range(2):
            out[0, row:row + 64] = ref[:, half * 128:(half + 1) * 128].reshape(64, 16, 128)
            row += 64


def relayout(tile, spot, parts, orbitals):
    def block(step, spot_ref):
        return ((spot_ref[3] + step * spot_ref[2] + 4) % 4, 0, 0)

    blocks = sum(8 * count + 1 for _, count in parts) + 128 * len(orbitals)
    return pl.pallas_call(
        functools.partial(relayout_body, parts),
        grid_spec=pltpu.PrefetchScalarGridSpec(
            num_scalar_prefetch=1,
            grid=(4,),
            in_specs=[pl.BlockSpec((16, 128, 128), block)] + [VMEM] * len(orbitals),
            out_specs=pl.BlockSpec((1, blocks, 16, 128), lambda step, spot_ref: (step, 0, 0, 0)),
            scratch_shapes=[pltpu.VMEM((2048, 128), F32)],
        ),
        out_shape=jax.ShapeDtypeStruct((4, blocks, 16, 128), BF16),
        name="relayout",
        compiler_params=pltpu.CompilerParams(vmem_limit_bytes=8 * 1024 * 1024),
        cost_estimate=pl.CostEstimate(flops=0, bytes_accessed=4 << 20, transcendentals=0),
    )(spot, tile, *orbitals)


def stack_body(start, first, a, b, c, out):
    blocks = out.shape[1] // 16
    out[0] = first[0, start:start + blocks].reshape(out.shape[1:])
    for i, ref in enumerate((a, b, c)):
        out[i + 1] = ref[start:start + blocks].reshape(out.shape[1:])


def product_body(count, h, spot_ref, t0, t1, t2, t3, orb, o1, o2, o3, out, rows, orbs):
    rp = 16 * count
    x, k, sign = spot_ref[0], spot_ref[1], spot_ref[2]
    for ref in (t0, t1, t2, t3):
        for i in range(4):
            code = jnp.max(ref[i, 8 * rp:8 * rp + 16, :].astype(F32)).astype(jnp.int32)
            m = code >> 3
            lane = pl.multiple_of((code & 7) * 128, 128)
            for e in range(4):
                towards = (x + sign * e + 4) % 4 if h == 0 else (x - sign * e + 4) % 4
                source = pl.multiple_of((((k + h) % 2) * 4 + towards) * rp, rp)
                rows[m, e * rp:(e + 1) * rp, pl.ds(lane, 128)] = ref[i, pl.ds(source, rp), :]
    orbs[0] = orb[...]
    for d, ref in enumerate((o1, o2, o3)):
        for half in range(2):
            start = ref.shape[0] - 128 + 64 * half
            orbs[d + 1, :, half * 128:(half + 1) * 128] = ref[start:start + 64].reshape(1024, 128)
    for d in range(4):
        place = d if h == 0 else (4 - d) % 4
        for m in range(2):
            acc = jnp.dot(rows[m], orbs[d], preferred_element_type=F32)
            for e in range(4):
                out[e, place, m] = acc[e * rp:(e + 1) * rp].astype(BF16)


def product(count, h, spot, tiles, orbs, after):
    rp = 16 * count
    return call(
        functools.partial(product_body, count, h),
        jax.ShapeDtypeStruct((4, 4, 2, rp, 256), BF16),
        [SMEM] + [VMEM] * 8,
        "product",
        (spot, *tiles, *orbs),
        after,
        scratch=[pltpu.VMEM((2, 4 * rp, 1024), BF16), pltpu.VMEM((4, 1024, 256), BF16)],
        flops=2 * 2 * 4 * rp * 1024 * 1024,
        nbytes=6 << 20,
        limit=14,
    )


def pair_body(a, b, ahead, behind):
    ahead[...] = (a[2].astype(F32) + b[2].astype(F32)).astype(BF16)
    behind[...] = (a[3].astype(F32) + b[3].astype(F32)).astype(BF16)


def relay_body(a, b, passing, out):
    out[...] = (a[1].astype(F32) + b[1].astype(F32) + passing[...].astype(F32)).astype(BF16)


def total_body(a, b, j1, j2, *outs):
    for d, out in enumerate(outs):
        value = a[0, d].astype(F32) + b[0, d].astype(F32)
        out[...] = (value + j1[d].astype(F32) + j2[d].astype(F32)).astype(BF16)


def fit_body(count, spot_ref, c0, c1, c2, c3, metric, fitted, s0, s1, s2, s3, coef, fit):
    x, k, sign, y = spot_ref[0], spot_ref[1], spot_ref[2], spot_ref[3]
    for d, ref in enumerate((c0, c1, c2, c3)):
        row = pl.multiple_of(((y + sign * d + 4) % 4) * 16, 16)
        for m in range(2):
            for uu in range(count):
                coef[m, pl.ds(row, 16), uu * 256:(uu + 1) * 256] = ref[m, uu * 16:(uu + 1) * 16, :]
    for m in range(2):
        high = metric[m].astype(BF16)
        low = (metric[m] - high.astype(F32)).astype(BF16)
        both = jnp.concatenate([high, low], axis=1)
        value = coef[m]
        fit[m] = jnp.dot(both, jnp.concatenate([value, value], axis=0), preferred_element_type=F32).astype(BF16)
    fitted[...] = fit[...]
    for e, out in enumerate((s0, s1, s2, s3)):
        for h in range(2):
            m = (k + h) % 2
            q = pl.multiple_of(((x + sign * e + 4) % 4) * 16, 16)
            out[h, 0] = fit[m, pl.ds(q, 16), :]
            out[h, 1] = coef[m, pl.ds(q, 16), :]


def fit_part(count, spot, pieces, metric, after):
    lanes = 256 * count
    shape = jax.ShapeDtypeStruct((2, 64, lanes), BF16)
    send = jax.ShapeDtypeStruct((2, 2, 16, lanes), BF16)
    return call(
        functools.partial(fit_body, count),
        [shape, send, send, send, send],
        [SMEM] + [VMEM] * 5,
        "fit",
        (spot, *pieces, metric),
        after,
        scratch=[pltpu.VMEM((2, 64, lanes), BF16), pltpu.VMEM((2, 64, lanes), BF16)],
        flops=2 * 2 * 64 * 128 * lanes,
        nbytes=1 << 20,
    )


def assemble_body(parts, *refs):
    out = refs[-1]
    for (offset, count), ref in zip(parts, refs[:-1]):
        for uu in range(count):
            for m in range(2):
                out[m, :, offset + uu, :] = ref[m, :, uu * 256:(uu + 1) * 256]


def exchange_body(parts, spot_ref, *refs):
    *outs, total = refs[-9:-4]
    wides = refs[-4:]
    x, k, sign = spot_ref[0], spot_ref[1], spot_ref[2]
    refs = refs[:-9]
    for part, (offset, count) in enumerate(parts):
        near, far = refs[4 * part:4 * part + 4], refs[-1]
        for e in range(4):
            for h in range(2):
                source = (x - sign * e + 4) % 4 if h == 0 else (x + sign * e + 4) % 4
                r = 2 * source + (k + h) % 2
                for uu in range(count):
                    row = pl.multiple_of((16 * r + offset + uu) * 16, 16)
                    for index, wide in enumerate(wides):
                        which, lane = index // 2, uu * 256 + index % 2 * 128
                        lanes, far_lanes = (slice(at, at + 128) for at in (lane, offset * 256 + lane))
                        value = near[e][0, which, :, lanes] if h == 0 else far[e, which, :, far_lanes]
                        wide[pl.ds(row, 16), :] = value.astype(F32)
    acc = jnp.zeros((128, 128), F32)
    for q in range(16):
        halves = [wide[pl.ds(q, 128, stride=16), :].astype(BF16) for wide in wides]
        a = jnp.concatenate(halves[:2], axis=1)
        b = jnp.concatenate(halves[2:], axis=1)
        acc = acc + lax.dot_general(a, b, (((1,), (1,)), ((), ())), preferred_element_type=F32)
    total[...] = acc
    for e, out in enumerate(outs):
        out[...] = total[pl.ds(pl.multiple_of(((x + sign * e + 4) % 4) * 32, 32), 32), :]


def on_device(tiles, tile_mu, tile_nu, orbitals, metric_inverse):
    row = lax.axis_index("row").astype(jnp.int32)
    col = lax.axis_index("col").astype(jnp.int32)
    x, k, y = row // 2, row % 2, col % 4
    sign = 1 - 2 * k
    spot = jnp.stack([x, k, sign, y, tile_mu[0] * 8 + tile_nu[0]])
    last = len(CHUNKS) - 1
    offsets = [sum(CHUNKS[:i]) for i in range(len(CHUNKS))]
    parts = list(zip(offsets, CHUNKS))

    shards, gathered, sums, fits = {}, {}, {}, {}
    groups = [parts[:1], parts[1:]]
    spread = []

    def over_y(group, held):
        with jax.named_scope("tiles_over_y"):
            spread.append((held, *[move(held[d], "y", d) for d in (1, 2, 3)]))

    def stack(i, after):
        with jax.named_scope("tiles_over_z"):
            start = 8 * (parts[i][0] - parts[min(i, 1)][0]) + max(i - 1, 0)
            shape = jax.ShapeDtypeStruct((4, (8 * parts[i][1] + 1) * 16, 128), BF16)
            body = functools.partial(stack_body, start)
            shards[i] = call(body, shape, [VMEM] * 4, "stack", spread[min(i, 1)], after, nbytes=1 << 20)

    def gather_z(i, after):
        with jax.named_scope("tiles_over_z"):
            near = gate(move(shards[i], "z", 1), after)
            across = move(gate(shards[i], [near]), "z", 3)
            gathered[i] = (shards[i], near, across, move(near, "z", 1))

    partial, got, blocks, arrived = {}, {}, {}, {}

    def multiply(i, after):
        with jax.named_scope("products"):
            others = product(CHUNKS[i], 1, spot, gathered[i], orbs, after)
            partial[i] = (product(CHUNKS[i], 0, spot, gathered[i], orbs, [others]), others)

    def sum_rows(i, after):
        mine, others = partial[i]
        with jax.named_scope("sum_cores"):
            twin = swap_core(others)
            shape = jax.ShapeDtypeStruct(mine.shape[1:], BF16)
            ahead, behind = call(pair_body, [shape] * 2, [VMEM] * 2, "pair", (mine, twin), after, nbytes=3 << 20)
        with jax.named_scope("sum_x"):
            passing, behind = move(ahead, "x", 1), move(behind, "x", 3)
            ahead = call(relay_body, shape, [VMEM] * 3, "relay", (mine, twin, passing), nbytes=2 << 20)
            got[i] = (mine, twin, behind, move(ahead, "x", 1))

    def coeffs(i):
        with jax.named_scope("sum_x"):
            shape = jax.ShapeDtypeStruct(got[i][0].shape[2:], BF16)
            blocks[i] = call(total_body, [shape] * 4, [VMEM] * 4, "total", got[i], nbytes=2 << 20)
        with jax.named_scope("coeffs_over_y"):
            blocks[i] = [blocks[i][0]] + [move(blocks[i][d], "y", -d) for d in (1, 2, 3)]

    def fit(i, after):
        with jax.named_scope("fit"):
            fits[i], *sends = fit_part(CHUNKS[i], spot, blocks[i], metric_inverse, after)
        with jax.named_scope("exchange_over_row"):
            arrived[i] = [sends[0]] + [move(sends[e], "x", e) for e in (1, 2, 3)]

    laid = [relayout(tiles[0], spot, group, held) for group, held in zip(groups, ([], [orbitals]))]
    over_y(groups[0], laid[0])
    stack(0, [laid[1]])
    over_y(groups[1], gate(laid[1], [shards[0]]))
    gather_z(0, [spread[1][3]])
    orbs = [orbitals, *spread[1][1:]]
    for i in range(last + 1):
        if i < last:
            stack(i + 1, gathered[i][2:])
        multiply(i, ([shards[i + 1]] if i < last else []) + (list(got[i - 1][2:]) if i > 0 else []))
        if i < last:
            gather_z(i + 1, [partial[i][0]])
        sum_rows(i, [gathered[i + 1][1]] if i < last else [])
        if i == 0:
            coeffs(0)
        else:
            coeffs(i)
            fit(i - 1, [blocks[i][0]])
    fit(last, arrived[last - 1][1:3] if last else [])

    with jax.named_scope("fitted_out"):
        fitted = call(
            functools.partial(assemble_body, parts),
            jax.ShapeDtypeStruct((2, 64, 16, 256), BF16),
            [VMEM] * len(parts),
            "assemble",
            [fits[i] for i in range(last + 1)],
            nbytes=2 << 20,
        )

    with jax.named_scope("exchange"):
        far = [jnp.stack([part[1] for part in arrived[i]]) for i in range(last + 1)]
        far = swap_core(jnp.concatenate(far, axis=3))
        pieces = [piece for i in range(last + 1) for piece in arrived[i]] + [far]
        blocks = call(
            functools.partial(exchange_body, parts),
            [jax.ShapeDtypeStruct((32, 128), F32)] * 4,
            [SMEM] + [VMEM] * len(pieces),
            "exchange",
            (spot, *pieces),
            scratch=[pltpu.VMEM((128, 128), F32)] + [pltpu.VMEM((2048, 128), F32)] * 4,
            flops=2 * 128 * 128 * 4096,
            nbytes=2 << 20,
        )
        total = blocks[0] + (move(blocks[1], "x", 1) + move(blocks[2], "x", 2) + move(blocks[3], "x", 3))
        keep = jnp.where(k == 0, total[:16], total[16:])
        got = swap_core(jnp.where(k == 0, total[16:], total[:16]))
        total = jnp.stack([jnp.where(k == 0, keep, got), jnp.where(k == 0, got, keep)])
        for axis, mask in (("y", 1), ("y", 2), ("z", 1), ("z", 2)):
            total = total + trade(total, axis, mask)
        exchange = total / 262144.0
    return fitted, exchange


def solution(mesh):
    return jax.shard_map(
        on_device,
        mesh=mesh,
        in_specs=(
            P(("row", "col"), None, None, None),
            P(("row", "col")),
            P(("row", "col")),
            P("row", "col"),
            P(),
        ),
        out_specs=(P(None, None, "row", "col"), P(None, "row", None)),
        check_vma=False,
    )
```

```python
import functools

import jax
import jax.numpy as jnp
from jax import lax
from jax.experimental import pallas as pl
from jax.experimental.pallas import tpu as pltpu
from jax.sharding import PartitionSpec as P

F32 = jnp.float32
BF16 = jnp.bfloat16

CHUNKS = (8, 8)

VMEM = pl.BlockSpec(memory_space=pltpu.VMEM)
SMEM = pl.BlockSpec(memory_space=pltpu.SMEM)
ANY = pl.BlockSpec(memory_space=pl.ANY)


def index(x, k, z, y):
    return ((x * 2 + k) * 4 + z) * 4 + y


def move(value, axis, step):
    pairs = []
    for x in range(4):
        for k in range(2):
            for z in range(4):
                for y in range(4):
                    to = dict(x=x, z=z, y=y)
                    to[axis] = (to[axis] + step * (1 - 2 * k)) % 4
                    pairs.append((index(x, k, z, y), index(to["x"], k, to["z"], to["y"])))
    return lax.ppermute(value, ("row", "col"), pairs)


def trade(value, axis, mask):
    pairs = [(c, c ^ (mask if axis == "y" else 4 * mask)) for c in range(16)]
    return lax.ppermute(value, "col", pairs)


def swap_core(value):
    return lax.ppermute(value, "row", [(r, r ^ 1) for r in range(8)])


def call(body, out_shape, in_specs, name, args, after=(), scratch=(), flops=0, nbytes=0, limit=8):
    given, marks = len(args), [mark(item) for item in after]

    def kernel(*refs):
        body(*refs[:given], *refs[given + len(marks):])

    return pl.pallas_call(
        kernel,
        out_shape=out_shape,
        in_specs=list(in_specs) + [VMEM] * len(marks),
        out_specs=jax.tree.map(lambda _: VMEM, out_shape),
        scratch_shapes=list(scratch),
        name=name,
        compiler_params=pltpu.CompilerParams(vmem_limit_bytes=limit * 1024 * 1024),
        cost_estimate=pl.CostEstimate(flops=flops, bytes_accessed=nbytes, transcendentals=0),
    )(*args, *marks)


def mark(item):
    item = item[(0,) * (item.ndim - 2)]
    return item[:16, :128]


def copy_body(source, out):
    out[...] = source[...]


def gate(value, after):
    shape = jax.ShapeDtypeStruct(value.shape, value.dtype)
    return call(copy_body, shape, [VMEM], "gate", (value,), after, nbytes=2 * value.size * 2)


def relayout_body(parts, spot_ref, x_ref, *refs):
    *orbitals, out, wide = refs
    wide[...] = x_ref[...].reshape(wide.shape).astype(F32)
    row = 0
    for offset, count in parts:
        for r in [2 * x + k for k in range(2) for x in range(4)]:
            for u in range(16 * r + offset, 16 * r + offset + count):
                out[0, row] = wide[pl.ds(u, 16, stride=128), :].astype(BF16)
                row += 1
        out[0, row] = jnp.full((16, 128), spot_ref[4].astype(F32), F32).astype(BF16)
        row += 1
    for ref in orbitals:
        for half in range(2):
            out[0, row:row + 64] = ref[:, half * 128:(half + 1) * 128].reshape(64, 16, 128)
            row += 64


def relayout(tile, spot, parts, orbitals):
    def block(step, spot_ref):
        return ((spot_ref[3] + step * spot_ref[2] + 4) % 4, 0, 0)

    blocks = sum(8 * count + 1 for _, count in parts) + 128 * len(orbitals)
    return pl.pallas_call(
        functools.partial(relayout_body, parts),
        grid_spec=pltpu.PrefetchScalarGridSpec(
            num_scalar_prefetch=1,
            grid=(4,),
            in_specs=[pl.BlockSpec((16, 128, 128), block)] + [VMEM] * len(orbitals),
            out_specs=pl.BlockSpec((1, blocks, 16, 128), lambda step, spot_ref: (step, 0, 0, 0)),
            scratch_shapes=[pltpu.VMEM((2048, 128), F32)],
        ),
        out_shape=jax.ShapeDtypeStruct((4, blocks, 16, 128), BF16),
        name="relayout",
        compiler_params=pltpu.CompilerParams(vmem_limit_bytes=8 * 1024 * 1024),
        cost_estimate=pl.CostEstimate(flops=0, bytes_accessed=4 << 20, transcendentals=0),
    )(spot, tile, *orbitals)


def stack_body(start, first, a, b, c, out):
    blocks = out.shape[1] // 16
    out[0] = first[0, start:start + blocks].reshape(out.shape[1:])
    for i, ref in enumerate((a, b, c)):
        out[i + 1] = ref[start:start + blocks].reshape(out.shape[1:])


def product_body(count, h, spot_ref, t0, t1, t2, t3, orb, o1, o2, o3, out, rows, orbs):
    rp = 16 * count
    x, k, sign = spot_ref[0], spot_ref[1], spot_ref[2]
    for ref in (t0, t1, t2, t3):
        for i in range(4):
            code = jnp.max(ref[i, 8 * rp:8 * rp + 16, :].astype(F32)).astype(jnp.int32)
            m = code >> 3
            lane = pl.multiple_of((code & 7) * 128, 128)
            for e in range(4):
                towards = (x + sign * e + 4) % 4 if h == 0 else (x - sign * e + 4) % 4
                source = pl.multiple_of((((k + h) % 2) * 4 + towards) * rp, rp)
                rows[m, e * rp:(e + 1) * rp, pl.ds(lane, 128)] = ref[i, pl.ds(source, rp), :]
    orbs[0] = orb[...]
    for d, ref in enumerate((o1, o2, o3)):
        for half in range(2):
            start = ref.shape[0] - 128 + 64 * half
            orbs[d + 1, :, half * 128:(half + 1) * 128] = ref[start:start + 64].reshape(1024, 128)
    for d in range(4):
        place = d if h == 0 else (4 - d) % 4
        for m in range(2):
            acc = jnp.dot(rows[m], orbs[d], preferred_element_type=F32)
            for e in range(4):
                out[e, place, m] = acc[e * rp:(e + 1) * rp].astype(BF16)


def product(count, h, spot, tiles, orbs, after):
    rp = 16 * count
    return call(
        functools.partial(product_body, count, h),
        jax.ShapeDtypeStruct((4, 4, 2, rp, 256), BF16),
        [SMEM] + [VMEM] * 8,
        "product",
        (spot, *tiles, *orbs),
        after,
        scratch=[pltpu.VMEM((2, 4 * rp, 1024), BF16), pltpu.VMEM((4, 1024, 256), BF16)],
        flops=2 * 2 * 4 * rp * 1024 * 1024,
        nbytes=6 << 20,
        limit=14,
    )


def pair_body(a, b, ahead, behind):
    ahead[...] = (a[2].astype(F32) + b[2].astype(F32)).astype(BF16)
    behind[...] = (a[3].astype(F32) + b[3].astype(F32)).astype(BF16)


def relay_body(a, b, passing, out):
    out[...] = (a[1].astype(F32) + b[1].astype(F32) + passing[...].astype(F32)).astype(BF16)


def total_body(a, b, j1, j2, *outs):
    for d, out in enumerate(outs):
        value = a[0, d].astype(F32) + b[0, d].astype(F32)
        out[...] = (value + j1[d].astype(F32) + j2[d].astype(F32)).astype(BF16)


def fit_body(count, spot_ref, c0, c1, c2, c3, metric, fitted, s0, s1, s2, s3, coef, fit):
    x, k, sign, y = spot_ref[0], spot_ref[1], spot_ref[2], spot_ref[3]
    for d, ref in enumerate((c0, c1, c2, c3)):
        row = pl.multiple_of(((y + sign * d + 4) % 4) * 16, 16)
        for m in range(2):
            for uu in range(count):
                coef[m, pl.ds(row, 16), uu * 256:(uu + 1) * 256] = ref[m, uu * 16:(uu + 1) * 16, :]
    for m in range(2):
        high = metric[m].astype(BF16)
        low = (metric[m] - high.astype(F32)).astype(BF16)
        both = jnp.concatenate([high, low], axis=1)
        value = coef[m]
        fit[m] = jnp.dot(both, jnp.concatenate([value, value], axis=0), preferred_element_type=F32).astype(BF16)
    fitted[...] = fit[...]
    for e, out in enumerate((s0, s1, s2, s3)):
        for h in range(2):
            m = (k + h) % 2
            q = pl.multiple_of(((x + sign * e + 4) % 4) * 16, 16)
            out[h, 0] = fit[m, pl.ds(q, 16), :]
            out[h, 1] = coef[m, pl.ds(q, 16), :]


def fit_part(count, spot, pieces, metric, after):
    lanes = 256 * count
    shape = jax.ShapeDtypeStruct((2, 64, lanes), BF16)
    send = jax.ShapeDtypeStruct((2, 2, 16, lanes), BF16)
    return call(
        functools.partial(fit_body, count),
        [shape, send, send, send, send],
        [SMEM] + [VMEM] * 5,
        "fit",
        (spot, *pieces, metric),
        after,
        scratch=[pltpu.VMEM((2, 64, lanes), BF16), pltpu.VMEM((2, 64, lanes), BF16)],
        flops=2 * 2 * 64 * 128 * lanes,
        nbytes=1 << 20,
    )


def assemble_body(parts, *refs):
    out = refs[-1]
    for (offset, count), ref in zip(parts, refs[:-1]):
        for uu in range(count):
            for m in range(2):
                out[m, :, offset + uu, :] = ref[m, :, uu * 256:(uu + 1) * 256]


def exchange_body(parts, spot_ref, *refs):
    *outs, total = refs[-9:-4]
    wides = refs[-4:]
    x, k, sign = spot_ref[0], spot_ref[1], spot_ref[2]
    refs = refs[:-9]
    for part, (offset, count) in enumerate(parts):
        near, far = refs[4 * part:4 * part + 4], refs[-1]
        for e in range(4):
            for h in range(2):
                source = (x - sign * e + 4) % 4 if h == 0 else (x + sign * e + 4) % 4
                r = 2 * source + (k + h) % 2
                for uu in range(count):
                    row = pl.multiple_of((16 * r + offset + uu) * 16, 16)
                    for index, wide in enumerate(wides):
                        which, lane = index // 2, uu * 256 + index % 2 * 128
                        lanes, far_lanes = (slice(at, at + 128) for at in (lane, offset * 256 + lane))
                        value = near[e][0, which, :, lanes] if h == 0 else far[e, which, :, far_lanes]
                        wide[pl.ds(row, 16), :] = value.astype(F32)
    acc = jnp.zeros((128, 128), F32)
    for q in range(16):
        halves = [wide[pl.ds(q, 128, stride=16), :].astype(BF16) for wide in wides]
        a = jnp.concatenate(halves[:2], axis=1)
        b = jnp.concatenate(halves[2:], axis=1)
        acc = acc + lax.dot_general(a, b, (((1,), (1,)), ((), ())), preferred_element_type=F32)
    total[...] = acc
    for e, out in enumerate(outs):
        out[...] = total[pl.ds(pl.multiple_of(((x + sign * e + 4) % 4) * 32, 32), 32), :]


def on_device(tiles, tile_mu, tile_nu, orbitals, metric_inverse):
    row = lax.axis_index("row").astype(jnp.int32)
    col = lax.axis_index("col").astype(jnp.int32)
    x, k, y = row // 2, row % 2, col % 4
    sign = 1 - 2 * k
    spot = jnp.stack([x, k, sign, y, tile_mu[0] * 8 + tile_nu[0]])
    last = len(CHUNKS) - 1
    offsets = [sum(CHUNKS[:i]) for i in range(len(CHUNKS))]
    parts = list(zip(offsets, CHUNKS))

    shards, gathered, sums, fits = {}, {}, {}, {}
    groups = [parts[:1], parts[1:]]
    spread = []

    def over_y(group, held):
        with jax.named_scope("tiles_over_y"):
            spread.append((held, *[move(held[d], "y", d) for d in (1, 2, 3)]))

    def stack(i, after):
        with jax.named_scope("tiles_over_z"):
            start = 8 * (parts[i][0] - parts[min(i, 1)][0]) + max(i - 1, 0)
            shape = jax.ShapeDtypeStruct((4, (8 * parts[i][1] + 1) * 16, 128), BF16)
            body = functools.partial(stack_body, start)
            shards[i] = call(body, shape, [VMEM] * 4, "stack", spread[min(i, 1)], after, nbytes=1 << 20)

    def gather_z(i, after):
        with jax.named_scope("tiles_over_z"):
            near = gate(move(shards[i], "z", 1), after)
            across = move(gate(shards[i], [near]), "z", 3)
            gathered[i] = (shards[i], near, across, move(near, "z", 1))

    partial, got, blocks, arrived = {}, {}, {}, {}

    def multiply(i, after):
        with jax.named_scope("products"):
            others = product(CHUNKS[i], 1, spot, gathered[i], orbs, after)
            partial[i] = (product(CHUNKS[i], 0, spot, gathered[i], orbs, [others]), others)

    def sum_rows(i, after):
        mine, others = partial[i]
        with jax.named_scope("sum_cores"):
            twin = swap_core(others)
            shape = jax.ShapeDtypeStruct(mine.shape[1:], BF16)
            ahead, behind = call(pair_body, [shape] * 2, [VMEM] * 2, "pair", (mine, twin), after, nbytes=3 << 20)
        with jax.named_scope("sum_x"):
            passing, behind = move(ahead, "x", 1), move(behind, "x", 3)
            ahead = call(relay_body, shape, [VMEM] * 3, "relay", (mine, twin, passing), nbytes=2 << 20)
            got[i] = (mine, twin, behind, move(ahead, "x", 1))

    def coeffs(i):
        with jax.named_scope("sum_x"):
            shape = jax.ShapeDtypeStruct(got[i][0].shape[2:], BF16)
            blocks[i] = call(total_body, [shape] * 4, [VMEM] * 4, "total", got[i], nbytes=2 << 20)
        with jax.named_scope("coeffs_over_y"):
            blocks[i] = [blocks[i][0]] + [move(blocks[i][d], "y", -d) for d in (1, 2, 3)]

    def fit(i, after):
        with jax.named_scope("fit"):
            fits[i], *sends = fit_part(CHUNKS[i], spot, blocks[i], metric_inverse, after)
        with jax.named_scope("exchange_over_row"):
            arrived[i] = [sends[0]] + [move(sends[e], "x", e) for e in (1, 2, 3)]

    laid = [relayout(tiles[0], spot, group, held) for group, held in zip(groups, ([], [orbitals]))]
    over_y(groups[0], laid[0])
    stack(0, [laid[1]])
    over_y(groups[1], gate(laid[1], [shards[0]]))
    gather_z(0, [spread[1][3]])
    orbs = [orbitals, *spread[1][1:]]
    for i in range(last + 1):
        if i < last:
            stack(i + 1, gathered[i][2:])
        multiply(i, ([shards[i + 1]] if i < last else []) + (list(got[i - 1][2:]) if i > 0 else []))
        if i < last:
            gather_z(i + 1, [partial[i][0]])
        sum_rows(i, [gathered[i + 1][1]] if i < last else [])
        if i == 0:
            coeffs(0)
        else:
            coeffs(i)
            fit(i - 1, [blocks[i][0]])
    fit(last, arrived[last - 1][1:2] if last else [])

    with jax.named_scope("fitted_out"):
        fitted = call(
            functools.partial(assemble_body, parts),
            jax.ShapeDtypeStruct((2, 64, 16, 256), BF16),
            [VMEM] * len(parts),
            "assemble",
            [fits[i] for i in range(last + 1)],
            nbytes=2 << 20,
        )

    with jax.named_scope("exchange"):
        far = [jnp.stack([part[1] for part in arrived[i]]) for i in range(last + 1)]
        far = swap_core(jnp.concatenate(far, axis=3))
        pieces = [piece for i in range(last + 1) for piece in arrived[i]] + [far]
        blocks = call(
            functools.partial(exchange_body, parts),
            [jax.ShapeDtypeStruct((32, 128), F32)] * 4,
            [SMEM] + [VMEM] * len(pieces),
            "exchange",
            (spot, *pieces),
            [fitted],
            scratch=[pltpu.VMEM((128, 128), F32)] + [pltpu.VMEM((2048, 128), F32)] * 4,
            flops=2 * 128 * 128 * 4096,
            nbytes=2 << 20,
        )
        total = blocks[0] + (move(blocks[1], "x", 1) + move(blocks[2], "x", 2) + move(blocks[3], "x", 3))
        keep = jnp.where(k == 0, total[:16], total[16:])
        got = swap_core(jnp.where(k == 0, total[16:], total[:16]))
        total = jnp.stack([jnp.where(k == 0, keep, got), jnp.where(k == 0, got, keep)])
        for axis, mask in (("y", 1), ("y", 2), ("z", 1), ("z", 2)):
            total = total + trade(total, axis, mask)
        exchange = total / 262144.0
    return fitted, exchange


def solution(mesh):
    return jax.shard_map(
        on_device,
        mesh=mesh,
        in_specs=(
            P(("row", "col"), None, None, None),
            P(("row", "col")),
            P(("row", "col")),
            P("row", "col"),
            P(),
        ),
        out_specs=(P(None, None, "row", "col"), P(None, "row", None)),
        check_vma=False,
    )
```
